32 devices in a mesh: gx: 8 (over z, x), yz: 4 (over y, core).
Axes of the slice: x: 2, y: 2, z: 4, core: 2. Of those that a mesh axis runs over, the one named last changes fastest.
Arguments:
- tensor_slabs: bfloat16 [512, 16, 1024], P('gx', 'yz'), may hold values from -6 to 6
- slab_counts: int32 [4], replicated, may hold values from 1 to 4, 8 in all
- column_scale: float32 [8, 1024], replicated, may hold values from -6 to 6
- samples: int32 [8, 256], replicated, may hold values from 0 to 1023
Outputs:
- basis_factor: float32 [512, 256], P('gx')
- core_tensor: bfloat16 [256, 16, 1024], P(None, 'yz', 'gx')
The draws below stay inside these ranges and needn't reach their ends.
Inputs may be any that keep to these rules, and one draw needn't show every extreme that they name: `slab_counts`: the counts sum to 8; the largest is exactly 4. Slots at or beyond an index's count hold no slab and are not read.
All inputs are finite; a program needn't handle non-finite values.
Results may differ from the reference program's by a relative error of at most 0.0057.
Values may be sent and summed in bfloat16 or wider, within the bound.
A program may use at most 64 MiB of HBM per device.

```python
import math
import jax
import jax.numpy as jnp
import numpy as np
from jax import lax

B = 1024
SKETCH = 256
SLOT_DEV = 4
NY = 8
SLOTS = 16
ROWS = 512
N_YZ = 4


def touch_ends(array, stream_key, least, top_value):
    longest = array.shape.index(max(array.shape))
    spots = []
    for shift in (0, 1):
        where = [jax.random.randint(jax.random.fold_in(stream_key, axis), (), 0, length) for axis, length in enumerate(array.shape)]
        where[longest] = (where[longest] + shift) % array.shape[longest]
        spots.append(tuple(where))
    return array.at[spots[0]].set(least).at[spots[1]].set(top_value)


def level_of(stream_key, shape, cuts, low, high):
    level = 1.0
    for dim, blocks in cuts:
        steps = jax.random.uniform(jax.random.fold_in(jax.random.fold_in(stream_key, 6), dim), (blocks,), jnp.float32, low / len(cuts), high / len(cuts))
        level = level * jnp.repeat(jnp.exp(steps), shape[dim] // blocks).reshape((-1,) + (1,) * (len(shape) - 1 - dim))
    return level


def split_up(number_of, total, bound, slope):
    loads = [(1 << 20) // math.isqrt(standing ** slope) + 1 for standing in range(2, number_of + 1)]
    rest, given = total - bound - (number_of - 1), [1] * (number_of - 1)
    while rest > 0:
        candidates = [i for i in range(number_of - 1) if given[i] < bound]
        mass, left = sum([loads[i] for i in candidates]), rest
        for i in candidates:
            extra = min(bound - given[i], max(1, left * loads[i] // mass), rest)
            given[i] = given[i] + extra
            rest = rest - extra
    return np.array([bound] + given)


def ragged(stream_key, count, total, most, lean):
    if count == 2:
        one = jax.random.randint(stream_key, (), max(1, total - most), min(most, total - 1) + 1)
        return jnp.stack([one, total - one])
    tallies = jnp.asarray(split_up(count, total, most, lean), jnp.int32)
    pairs = (count - 1) // 2
    source_of, sink = tallies[1:1 + 2 * pairs:2], tallies[2:2 + 2 * pairs:2]
    room = jnp.minimum(source_of - 1, most - sink)
    shifted = jax.random.randint(jax.random.fold_in(stream_key, 1), (pairs,), 0, 1 << 20) % (room + 1)
    tallies = tallies.at[1:1 + 2 * pairs:2].set(source_of - shifted).at[2:2 + 2 * pairs:2].set(sink + shifted)
    return tallies[jax.random.permutation(jax.random.fold_in(stream_key, 2), count)]


def centred(own_key, shape, spread, limit, cuts=(), kind=jnp.bfloat16):
    array = jax.random.normal(own_key, shape, jnp.float32) * spread
    if len(cuts) > 0:
        array = level_of(own_key, shape, cuts, -0.22, 0.18) * array
    return jnp.clip(array, min=-limit, max=limit).astype(kind)


def setup_inputs(seed: int = 0) -> dict:
    splits = jax.random.split(jax.random.key(seed), 5)
    tensor_slabs = centred(splits[0], (ROWS, SLOTS, B), 1.0, 6.0, ((0, 8), (1, 4)))
    slab_counts = ragged(splits[1], N_YZ, NY, SLOT_DEV, 2).astype(jnp.int32)
    column_scale = centred(splits[2], (NY, B), 1.0, 6.0, (), jnp.float32)
    samples = touch_ends(jax.random.randint(splits[3], (NY, SKETCH), 0, B), jax.random.fold_in(splits[3], 1), 0, B - 1).astype(jnp.int32)
    return {"tensor_slabs": tensor_slabs, "slab_counts": slab_counts, "column_scale": column_scale, "samples": samples}


def hadamard_columns(picked, length):
    index_rows = jnp.arange(length, dtype=jnp.int32)[:, None]
    picked_row = picked.astype(jnp.int32)[None, :]
    parity = jnp.zeros((length, picked.shape[0]), jnp.int32)
    for bit_place in range(length.bit_length() - 1):
        parity = parity + jnp.bitwise_and(jnp.right_shift(index_rows, bit_place), 1) * jnp.bitwise_and(jnp.right_shift(picked_row, bit_place), 1)
    return (1 - 2 * (parity % 2)).astype(jnp.bfloat16)

def reference(tensor_slabs, slab_counts, column_scale, samples):
    counts = slab_counts.astype(jnp.int32)
    offsets = jnp.cumsum(counts).astype(jnp.int32) - counts
    pad_scale = jnp.concatenate([column_scale, jnp.zeros((SLOT_DEV, B), column_scale.dtype)], 0)
    pad_samples = jnp.concatenate([samples.astype(jnp.int32), jnp.zeros((SLOT_DEV, SKETCH), jnp.int32)], 0)

    def add_slab(total, slot_number):
        device_number = slot_number // SLOT_DEV
        position = slot_number % SLOT_DEV
        slab_index = offsets[device_number] + position
        alive = (position < counts[device_number]).astype(total.dtype)
        piece = lax.dynamic_index_in_dim(tensor_slabs, slot_number, 1, keepdims=False)
        scaled = (piece.astype(pad_scale.dtype) * pad_scale[slab_index][None, :]).astype(jnp.bfloat16)
        hadamard_part = hadamard_columns(pad_samples[slab_index], B)
        return (total + alive * jnp.dot(scaled.astype(jnp.float32), hadamard_part.astype(jnp.float32), preferred_element_type=jnp.float32).astype(total.dtype), None)
    start = jnp.zeros((ROWS, SKETCH), jnp.float32)
    summed = lax.scan(add_slab, start, jnp.arange(SLOTS, dtype=jnp.int32))[0]
    sketch = summed * (1.0 / math.sqrt(NY * B))
    gram_matrix = jnp.dot(sketch.T, sketch, precision=lax.Precision.HIGHEST)
    cholesky_factor = jnp.linalg.cholesky(gram_matrix)
    basis_factor = lax.linalg.triangular_solve(cholesky_factor, sketch, left_side=False, lower=True, transpose_a=True)
    factor_bf = basis_factor.astype(jnp.bfloat16)
    flattened = tensor_slabs.reshape(ROWS, SLOTS * B)
    projected = jnp.dot(factor_bf.T.astype(jnp.float32), flattened.astype(jnp.float32), preferred_element_type=jnp.float32).reshape(SKETCH, SLOTS, B)
    slot_numbers = jnp.arange(SLOTS, dtype=jnp.int32)
    slot_alive = (slot_numbers % SLOT_DEV < counts[slot_numbers // SLOT_DEV]).astype(projected.dtype)
    core_tensor = (projected * slot_alive[None, :, None]).astype(jnp.bfloat16)
    return (basis_factor, core_tensor)
```

```python
import functools
import math

import jax
import jax.numpy as jnp
from jax import lax
from jax.experimental import pallas as pl
from jax.experimental.pallas import tpu as pltpu
from jax.sharding import PartitionSpec as P

MESH = pl.DeviceIdType.MESH
HIGHEST = lax.Precision.HIGHEST
F32 = jnp.float32
BF16 = jnp.bfloat16
LOW_BITS = 5
CORES = 2
PANEL = 64


def signs(index_count, picked):
    shared = jnp.bitwise_and(
        lax.broadcasted_iota(jnp.int32, (index_count, picked.shape[1]), 0), picked
    )
    for step in (16, 8, 4, 2, 1):
        shared = jnp.bitwise_xor(shared, jnp.right_shift(shared, step))
    return (1 - 2 * jnp.bitwise_and(shared, 1)).astype(F32)


def sketch_kernel(
    n_gx, n_yz, slab_total, moves,
    counts_ref, slabs_ref, scale_ref, samples_ref, *rest,
):
    sketch_ref = rest[0]
    if moves:
        moved_ref = rest[1]
        a2a_send, a2a_recv, own_sem = rest[-3:]
        rest = rest[:1] + rest[2:-3]
    (
        hada, part, arrived, rs_send, rs_recv, gx_send, gx_recv, y_send, y_recv, c_send, c_recv
    ) = rest[1:]
    gx, yz = lax.axis_index("gx"), lax.axis_index("yz")
    slots, rows, width = slabs_ref.shape
    n_y = n_yz // CORES
    core = yz % CORES
    y_pos = yz // CORES
    own_cols = width // n_gx
    chunk = rows // n_yz

    def gx_peer(step):
        return lax.rem(gx + step, n_gx)

    def yz_peer(step):
        return lax.rem(yz + step, n_yz)

    barrier = pltpu.get_barrier_semaphore()
    for step in range(1, n_gx):
        pl.semaphore_signal(barrier, inc=1, device_id=(gx_peer(step), yz), device_id_type=MESH)
    for step in range(1, n_yz):
        pl.semaphore_signal(barrier, inc=1, device_id=(gx, yz_peer(step)), device_id_type=MESH)
    pl.semaphore_wait(barrier, n_gx + n_yz - 2)

    def columns_of(index):
        return pl.ds(pl.multiple_of(index * own_cols, own_cols), own_cols)

    def rows_of(index):
        return pl.ds(pl.multiple_of(index * rows, rows), rows)

    a2a = []
    if moves:
        own_copy = pltpu.make_async_copy(
            slabs_ref.at[:, :, columns_of(gx)], moved_ref.at[:, rows_of(gx), :], own_sem
        )
        own_copy.start()
        for step in range(1, n_gx):
            peer = gx_peer(step)
            copy = pltpu.make_async_remote_copy(
                src_ref=slabs_ref.at[:, :, columns_of(peer)],
                dst_ref=moved_ref.at[:, rows_of(gx), :],
                send_sem=a2a_send.at[step - 1],
                recv_sem=a2a_recv.at[step - 1],
                device_id=(peer, yz),
                device_id_type=MESH,
            )
            copy.start()
            a2a.append(copy)

    offset = jnp.int32(0)
    own_count = jnp.int32(0)
    for group in range(counts_ref.shape[0]):
        count = counts_ref[group]
        offset = offset + jnp.where(group < yz, count, 0)
        own_count = own_count + jnp.where(group == yz, count, 0)

    low = 1 << LOW_BITS
    high = width // low
    total = None
    for slot in range(slots):
        slab = jnp.minimum(offset + slot, slab_total - 1)
        alive = (slot < own_count).astype(F32)
        picked = samples_ref[pl.ds(slab, 1), :]
        high_sign = signs(high, jnp.right_shift(picked, LOW_BITS))
        low_sign = signs(low, jnp.bitwise_and(picked, low - 1))
        for top in range(high):
            hada[top * low : (top + 1) * low, :] = (high_sign[top : top + 1, :] * low_sign).astype(BF16)
        scale = scale_ref[pl.ds(slab, 1), :] * alive
        scaled = (slabs_ref[slot].astype(F32) * scale).astype(BF16)
        term = jnp.dot(scaled, hada[...], preferred_element_type=F32)
        total = term if total is None else total + term
    part[...] = total * (1.0 / math.sqrt(slab_total * width))

    def chunk_of(index):
        return pl.ds(pl.multiple_of(index * chunk, chunk), chunk)

    reduce = []
    for step in range(1, n_yz):
        peer = yz_peer(step)
        copy = pltpu.make_async_remote_copy(
            src_ref=part.at[chunk_of(peer)],
            dst_ref=arrived.at[step - 1],
            send_sem=rs_send.at[step - 1],
            recv_sem=rs_recv.at[step - 1],
            device_id=(gx, peer),
            device_id_type=MESH,
        )
        copy.start()
        reduce.append(copy)
    own = part[chunk_of(yz)]
    for step in range(1, n_yz):
        reduce[step - 1].wait_recv()
        own = own + arrived[step - 1]

    def place(gx_index, yz_index):
        start = gx_index * rows + yz_index * chunk
        return sketch_ref.at[pl.ds(pl.multiple_of(start, chunk), chunk)]

    place(gx, yz)[...] = own
    sent = []
    over_gx = []
    for step in range(1, n_gx):
        copy = pltpu.make_async_remote_copy(
            src_ref=place(gx, yz),
            dst_ref=place(gx, yz),
            send_sem=gx_send.at[step - 1],
            recv_sem=gx_recv.at[step - 1],
            device_id=(gx_peer(step), yz),
            device_id_type=MESH,
        )
        copy.start()
        over_gx.append(copy)

    def to_y(gx_index, slot):
        for step in range(1, n_y):
            peer = lax.rem(y_pos + step, n_y) * CORES + core
            copy = pltpu.make_async_remote_copy(
                src_ref=place(gx_index, yz),
                dst_ref=place(gx_index, yz),
                send_sem=y_send.at[step - 1, slot],
                recv_sem=y_recv.at[step - 1, slot],
                device_id=(gx, peer),
                device_id_type=MESH,
            )
            copy.start()
            over_y.append(copy)

    def to_core(gx_index, yz_index, y_step, slot):
        copy = pltpu.make_async_remote_copy(
            src_ref=place(gx_index, yz_index),
            dst_ref=place(gx_index, yz_index),
            send_sem=c_send.at[y_step, slot],
            recv_sem=c_recv.at[y_step, slot],
            device_id=(gx, y_pos * CORES + 1 - core),
            device_id_type=MESH,
        )
        copy.start()
        over_core.append(copy)

    over_y = []
    over_core = []
    to_y(gx, 0)
    to_core(gx, yz, 0, 0)
    for step in range(1, n_gx):
        over_gx[step - 1].wait_recv()
        source = lax.rem(gx + n_gx - step, n_gx)
        to_y(source, step)
        to_core(source, yz, 0, step)
    for slot in range(n_gx):
        source = lax.rem(gx + n_gx - slot, n_gx)
        for step in range(1, n_y):
            over_y[slot * (n_y - 1) + step - 1].wait_recv()
            from_yz = lax.rem(y_pos + n_y - step, n_y) * CORES + core
            to_core(source, from_yz, step, slot)
    for copy in over_core:
        copy.wait()
    for copy in over_y + over_gx + reduce:
        copy.wait_send()
    for copy in a2a:
        copy.wait()
    if moves:
        own_copy.wait()


def factor_kernel(counts_ref, sketch_ref, moved_ref, basis_ref, core_ref, work):
    gx, yz = lax.axis_index("gx"), lax.axis_index("yz")
    rank = sketch_ref.shape[1]
    slots = moved_ref.shape[0]
    own_rows = basis_ref.shape[0]
    lanes, tile = 128, 8
    gram = lax.dot_general(
        sketch_ref[...], sketch_ref[...], (((0,), (0,)), ((), ())),
        precision=HIGHEST, preferred_element_type=F32,
    )
    work[:, :rank] = gram
    work[:, rank:] = (
        lax.broadcasted_iota(jnp.int32, (rank, rank), 0)
        == lax.broadcasted_iota(jnp.int32, (rank, rank), 1)
    ).astype(F32)
    sub = lax.broadcasted_iota(jnp.int32, (tile, lanes), 0)
    full = (tile, lanes)

    for start in range(0, rank, PANEL):
        end = min(start + PANEL, rank)
        for row in range(start, end, tile):
            at = row // lanes
            first = row % lanes
            used = list(range(at, rank // lanes)) + list(range(rank // lanes, rank // lanes + at + 1))
            block = work[row : row + tile, at * lanes : (at + 1) * lanes]
            g = [[None] * tile for _ in range(tile)]
            for j in range(tile):
                column = jnp.broadcast_to(block[:, first + j : first + j + 1], full)
                for i in range(j, tile):
                    g[i][j] = jnp.broadcast_to(column[i : i + 1, :], full)
            l = [[None] * tile for _ in range(tile)]
            v = [[None] * tile for _ in range(tile)]
            for j in range(tile):
                inverse = lax.rsqrt(g[j][j])
                v[j][j] = inverse
                for i in range(j + 1, tile):
                    l[i][j] = g[i][j] * inverse
                for i in range(j + 1, tile):
                    for k in range(j + 1, i + 1):
                        g[i][k] = g[i][k] - l[i][j] * l[k][j]
                for k in range(j):
                    inner = l[j][k] * v[k][k]
                    for m in range(k + 1, j):
                        inner = inner + l[j][m] * v[m][k]
                    v[j][k] = -inverse * inner
            v_columns = []
            for j in range(tile):
                column = jnp.zeros(full, F32)
                for i in range(j, tile):
                    column = jnp.where(sub == i, v[i][j], column)
                v_columns.append(column)
            spread = {}
            for n in used:
                there = work[row : row + tile, n * lanes : (n + 1) * lanes]
                done = v_columns[0] * jnp.broadcast_to(there[0:1, :], full)
                for j in range(1, tile):
                    done = done + v_columns[j] * jnp.broadcast_to(there[j : j + 1, :], full)
                work[row : row + tile, n * lanes : (n + 1) * lanes] = done
                spread[n] = [jnp.broadcast_to(done[j : j + 1, :], full) for j in range(tile)]
            for below in range(row + tile, end, tile):
                there = work[below : below + tile, at * lanes : (at + 1) * lanes]
                raw = [
                    jnp.broadcast_to(there[:, first + j : first + j + 1], full) for j in range(tile)
                ]
                left = []
                for j in range(tile):
                    value = raw[0] * v[j][0]
                    for k in range(1, j + 1):
                        value = value + raw[k] * v[j][k]
                    left.append(value)
                for n in used:
                    value = work[below : below + tile, n * lanes : (n + 1) * lanes]
                    for j in range(tile):
                        value = value - left[j] * spread[n][j]
                    work[below : below + tile, n * lanes : (n + 1) * lanes] = value
        if end < rank:
            from_lane = end // lanes * lanes
            left = work[start:end, from_lane:rank]
            right = work[start:end, from_lane:]
            update = lax.dot_general(
                left, right, (((0,), (0,)), ((), ())), precision=HIGHEST, preferred_element_type=F32
            )
            work[end:, from_lane:] = work[end:, from_lane:] - update[end - from_lane :, :]

    keep = (
        lax.broadcasted_iota(jnp.int32, (rank, rank), 0)
        >= lax.broadcasted_iota(jnp.int32, (rank, rank), 1)
    )
    inverse = jnp.where(keep, work[:, rank:], 0.0)
    basis_ref[...] = lax.dot_general(
        sketch_ref[pl.ds(pl.multiple_of(gx * own_rows, own_rows), own_rows), :], inverse,
        (((1,), (1,)), ((), ())), precision=HIGHEST, preferred_element_type=F32,
    )
    factor = lax.dot_general(
        inverse, sketch_ref[...], (((1,), (1,)), ((), ())),
        precision=HIGHEST, preferred_element_type=F32,
    ).astype(BF16)
    own_count = counts_ref[yz]
    for slot in range(slots):
        alive = (slot < own_count).astype(F32)
        projected = jnp.dot(factor, moved_ref[slot], preferred_element_type=F32)
        core_ref[slot] = (projected * alive).astype(BF16)


def local(n_gx, n_yz, tensor_slabs, slab_counts, column_scale, samples):
    rows, slots, width = tensor_slabs.shape
    rank = samples.shape[1]
    slab_total = column_scale.shape[0]
    n_y = n_yz // CORES
    chunk = rows // n_yz
    own_cols = width // n_gx
    vmem = pl.BlockSpec(memory_space=pltpu.VMEM)
    smem = pl.BlockSpec(memory_space=pltpu.SMEM)
    dma = pltpu.SemaphoreType.DMA
    moves = own_cols % 128 == 0
    found = pl.pallas_call(
        functools.partial(sketch_kernel, n_gx, n_yz, slab_total, moves),
        out_shape=(
            jax.ShapeDtypeStruct((rows * n_gx, rank), F32),
            jax.ShapeDtypeStruct((slots, rows * n_gx, own_cols), BF16),
        )[: 1 + moves],
        in_specs=[smem, vmem, vmem, vmem],
        out_specs=(vmem, vmem)[: 1 + moves],
        scratch_shapes=[
            pltpu.VMEM((width, rank), BF16),
            pltpu.VMEM((rows, rank), F32),
            pltpu.VMEM((n_yz - 1, chunk, rank), F32),
            dma((n_yz - 1,)), dma((n_yz - 1,)),
            dma((n_gx - 1,)), dma((n_gx - 1,)),
            dma((max(n_y - 1, 1), n_gx)), dma((max(n_y - 1, 1), n_gx)),
            dma((n_y, n_gx)), dma((n_y, n_gx)),
        ] + ([dma((n_gx - 1,)), dma((n_gx - 1,)), dma(())] if moves else []),
        compiler_params=pltpu.CompilerParams(
            collective_id=0, has_side_effects=True, vmem_limit_bytes=32 << 20
        ),
    )(slab_counts, jnp.transpose(tensor_slabs, (1, 0, 2)), column_scale, samples)
    sketch = found[0]
    if moves:
        moved = found[1]
    else:
        moved = jnp.transpose(
            lax.all_to_all(tensor_slabs, "gx", split_axis=2, concat_axis=0, tiled=True), (1, 0, 2)
        )
    basis_factor, core = pl.pallas_call(
        factor_kernel,
        out_shape=(
            jax.ShapeDtypeStruct((rows, rank), F32),
            jax.ShapeDtypeStruct((slots, rank, own_cols), BF16),
        ),
        in_specs=[smem, vmem, vmem],
        out_specs=(vmem, vmem),
        scratch_shapes=[pltpu.VMEM((rank, 2 * rank), F32)],
        compiler_params=pltpu.CompilerParams(vmem_limit_bytes=32 << 20),
    )(slab_counts, sketch, moved)
    return basis_factor, jnp.transpose(core, (1, 0, 2))


def solution(mesh):
    placed = (P("gx", "yz", None), P(), P(), P())
    return jax.shard_map(
        functools.partial(local, mesh.shape["gx"], mesh.shape["yz"]),
        mesh=mesh,
        in_specs=placed,
        out_specs=(P("gx", None), P(None, "yz", "gx")),
        check_vma=False,
    )
```

```python
import functools
import math

import jax
import jax.numpy as jnp
from jax import lax
from jax.experimental import pallas as pl
from jax.experimental.pallas import tpu as pltpu
from jax.sharding import PartitionSpec as P

MESH = pl.DeviceIdType.MESH
HIGHEST = lax.Precision.HIGHEST
F32 = jnp.float32
BF16 = jnp.bfloat16
LOW_BITS = 5
CORES = 2
PANEL = 64


def signs(index_count, picked):
    shared = jnp.bitwise_and(
        lax.broadcasted_iota(jnp.int32, (index_count, picked.shape[1]), 0), picked
    )
    for step in (16, 8, 4, 2, 1):
        shared = jnp.bitwise_xor(shared, jnp.right_shift(shared, step))
    return (1 - 2 * jnp.bitwise_and(shared, 1)).astype(F32)


def sketch_kernel(
    n_gx, n_yz, slab_total, moves,
    counts_ref, slabs_ref, scale_ref, samples_ref, *rest,
):
    if moves:
        moved_ref, a2a_send, a2a_recv, own_sem = rest[-4:]
        rest = rest[:-4]
    else:
        moved_ref = rest[0]
        rest = rest[1:]
    (
        basis_ref, core_ref, sketch_ref, work, hada, part, arrived,
        rs_send, rs_recv, gx_send, gx_recv, y_send, y_recv, c_send, c_recv,
    ) = rest
    gx, yz = lax.axis_index("gx"), lax.axis_index("yz")
    slots, rows, width = slabs_ref.shape
    n_y = n_yz // CORES
    core = yz % CORES
    y_pos = yz // CORES
    own_cols = width // n_gx
    chunk = rows // n_yz

    def gx_peer(step):
        return lax.rem(gx + step, n_gx)

    def yz_peer(step):
        return lax.rem(yz + step, n_yz)

    barrier = pltpu.get_barrier_semaphore()
    for step in range(1, n_gx):
        pl.semaphore_signal(barrier, inc=1, device_id=(gx_peer(step), yz), device_id_type=MESH)
    for step in range(1, n_yz):
        pl.semaphore_signal(barrier, inc=1, device_id=(gx, yz_peer(step)), device_id_type=MESH)
    pl.semaphore_wait(barrier, n_gx + n_yz - 2)

    def columns_of(index):
        return pl.ds(pl.multiple_of(index * own_cols, own_cols), own_cols)

    def rows_of(index):
        return pl.ds(pl.multiple_of(index * rows, rows), rows)

    offset = jnp.int32(0)
    own_count = jnp.int32(0)
    for group in range(counts_ref.shape[0]):
        count = counts_ref[group]
        offset = offset + jnp.where(group < yz, count, 0)
        own_count = own_count + jnp.where(group == yz, count, 0)

    low = 1 << LOW_BITS
    high = width // low
    total = None
    for slot in range(slots):
        slab = jnp.minimum(offset + slot, slab_total - 1)
        alive = (slot < own_count).astype(F32)
        picked = samples_ref[pl.ds(slab, 1), :]
        high_sign = signs(high, jnp.right_shift(picked, LOW_BITS))
        low_sign = signs(low, jnp.bitwise_and(picked, low - 1))
        for top in range(high):
            hada[top * low : (top + 1) * low, :] = (high_sign[top : top + 1, :] * low_sign).astype(BF16)
        scale = scale_ref[pl.ds(slab, 1), :] * alive
        scaled = (slabs_ref[slot].astype(F32) * scale).astype(BF16)
        term = jnp.dot(scaled, hada[...], preferred_element_type=F32)
        total = term if total is None else total + term
    part[...] = total * (1.0 / math.sqrt(slab_total * width))

    def chunk_of(index):
        return pl.ds(pl.multiple_of(index * chunk, chunk), chunk)

    reduce = []
    for step in range(1, n_yz):
        peer = yz_peer(step)
        copy = pltpu.make_async_remote_copy(
            src_ref=part.at[chunk_of(peer)],
            dst_ref=arrived.at[step - 1],
            send_sem=rs_send.at[step - 1],
            recv_sem=rs_recv.at[step - 1],
            device_id=(gx, peer),
            device_id_type=MESH,
        )
        copy.start()
        reduce.append(copy)
    own = part[chunk_of(yz)]
    for step in range(1, n_yz):
        reduce[step - 1].wait_recv()
        own = own + arrived[step - 1]

    def place(gx_index, yz_index):
        start = gx_index * rows + yz_index * chunk
        return sketch_ref.at[pl.ds(pl.multiple_of(start, chunk), chunk)]

    place(gx, yz)[...] = own
    over_gx = []
    for step in range(1, n_gx):
        copy = pltpu.make_async_remote_copy(
            src_ref=place(gx, yz),
            dst_ref=place(gx, yz),
            send_sem=gx_send.at[step - 1],
            recv_sem=gx_recv.at[step - 1],
            device_id=(gx_peer(step), yz),
            device_id_type=MESH,
        )
        copy.start()
        over_gx.append(copy)

    def to_y(gx_index, slot):
        for step in range(1, n_y):
            peer = lax.rem(y_pos + step, n_y) * CORES + core
            copy = pltpu.make_async_remote_copy(
                src_ref=place(gx_index, yz),
                dst_ref=place(gx_index, yz),
                send_sem=y_send.at[step - 1, slot],
                recv_sem=y_recv.at[step - 1, slot],
                device_id=(gx, peer),
                device_id_type=MESH,
            )
            copy.start()
            over_y.append(copy)

    def to_core(gx_index, yz_index, y_step, slot):
        copy = pltpu.make_async_remote_copy(
            src_ref=place(gx_index, yz_index),
            dst_ref=place(gx_index, yz_index),
            send_sem=c_send.at[y_step, slot],
            recv_sem=c_recv.at[y_step, slot],
            device_id=(gx, y_pos * CORES + 1 - core),
            device_id_type=MESH,
        )
        copy.start()
        over_core.append(copy)

    over_y = []
    over_core = []
    to_y(gx, 0)
    to_core(gx, yz, 0, 0)
    for step in range(1, n_gx):
        over_gx[step - 1].wait_recv()
        source = lax.rem(gx + n_gx - step, n_gx)
        to_y(source, step)
        to_core(source, yz, 0, step)
    for slot in range(n_gx):
        source = lax.rem(gx + n_gx - slot, n_gx)
        for step in range(1, n_y):
            over_y[slot * (n_y - 1) + step - 1].wait_recv()
            from_yz = lax.rem(y_pos + n_y - step, n_y) * CORES + core
            to_core(source, from_yz, step, slot)
    a2a = []
    if moves:
        own_copy = pltpu.make_async_copy(
            slabs_ref.at[:, :, columns_of(gx)], moved_ref.at[:, rows_of(gx), :], own_sem
        )
        own_copy.start()
        for step in range(1, n_gx):
            peer = gx_peer(step)
            copy = pltpu.make_async_remote_copy(
                src_ref=slabs_ref.at[:, :, columns_of(peer)],
                dst_ref=moved_ref.at[:, rows_of(gx), :],
                send_sem=a2a_send.at[step - 1],
                recv_sem=a2a_recv.at[step - 1],
                device_id=(peer, yz),
                device_id_type=MESH,
            )
            copy.start()
            a2a.append(copy)
    for copy in over_core:
        copy.wait()
    for copy in over_y + over_gx + reduce:
        copy.wait_send()
    factor = factorise(sketch_ref, basis_ref, work)
    for copy in a2a:
        copy.wait()
    if moves:
        own_copy.wait()
    for slot in range(slots):
        alive = (slot < own_count).astype(F32)
        projected = jnp.dot(factor, moved_ref[slot], preferred_element_type=F32)
        core_ref[slot] = (projected * alive).astype(BF16)


def factorise(sketch_ref, basis_ref, work):
    gx = lax.axis_index("gx")
    rank = sketch_ref.shape[1]
    own_rows = basis_ref.shape[0]
    lanes, tile = 128, 8
    gram = lax.dot_general(
        sketch_ref[...], sketch_ref[...], (((0,), (0,)), ((), ())),
        precision=HIGHEST, preferred_element_type=F32,
    )
    work[:, :rank] = gram
    work[:, rank:] = (
        lax.broadcasted_iota(jnp.int32, (rank, rank), 0)
        == lax.broadcasted_iota(jnp.int32, (rank, rank), 1)
    ).astype(F32)
    sub = lax.broadcasted_iota(jnp.int32, (tile, lanes), 0)
    full = (tile, lanes)

    for start in range(0, rank, PANEL):
        end = min(start + PANEL, rank)
        for row in range(start, end, tile):
            at = row // lanes
            first = row % lanes
            used = list(range(at, rank // lanes)) + list(range(rank // lanes, rank // lanes + at + 1))
            block = work[row : row + tile, at * lanes : (at + 1) * lanes]
            g = [[None] * tile for _ in range(tile)]
            for j in range(tile):
                column = jnp.broadcast_to(block[:, first + j : first + j + 1], full)
                for i in range(j, tile):
                    g[i][j] = jnp.broadcast_to(column[i : i + 1, :], full)
            l = [[None] * tile for _ in range(tile)]
            v = [[None] * tile for _ in range(tile)]
            for j in range(tile):
                inverse = lax.rsqrt(g[j][j])
                v[j][j] = inverse
                for i in range(j + 1, tile):
                    l[i][j] = g[i][j] * inverse
                for i in range(j + 1, tile):
                    for k in range(j + 1, i + 1):
                        g[i][k] = g[i][k] - l[i][j] * l[k][j]
                for k in range(j):
                    inner = l[j][k] * v[k][k]
                    for m in range(k + 1, j):
                        inner = inner + l[j][m] * v[m][k]
                    v[j][k] = -inverse * inner
            v_columns = []
            for j in range(tile):
                column = jnp.zeros(full, F32)
                for i in range(j, tile):
                    column = jnp.where(sub == i, v[i][j], column)
                v_columns.append(column)
            spread = {}
            for n in used:
                there = work[row : row + tile, n * lanes : (n + 1) * lanes]
                done = v_columns[0] * jnp.broadcast_to(there[0:1, :], full)
                for j in range(1, tile):
                    done = done + v_columns[j] * jnp.broadcast_to(there[j : j + 1, :], full)
                work[row : row + tile, n * lanes : (n + 1) * lanes] = done
                spread[n] = [jnp.broadcast_to(done[j : j + 1, :], full) for j in range(tile)]
            for below in range(row + tile, end, tile):
                there = work[below : below + tile, at * lanes : (at + 1) * lanes]
                raw = [
                    jnp.broadcast_to(there[:, first + j : first + j + 1], full) for j in range(tile)
                ]
                left = []
                for j in range(tile):
                    value = raw[0] * v[j][0]
                    for k in range(1, j + 1):
                        value = value + raw[k] * v[j][k]
                    left.append(value)
                for n in used:
                    value = work[below : below + tile, n * lanes : (n + 1) * lanes]
                    for j in range(tile):
                        value = value - left[j] * spread[n][j]
                    work[below : below + tile, n * lanes : (n + 1) * lanes] = value
        if end < rank:
            from_lane = end // lanes * lanes
            left = work[start:end, from_lane:rank]
            right = work[start:end, from_lane:]
            update = lax.dot_general(
                left, right, (((0,), (0,)), ((), ())), precision=HIGHEST, preferred_element_type=F32
            )
            work[end:, from_lane:] = work[end:, from_lane:] - update[end - from_lane :, :]

    keep = (
        lax.broadcasted_iota(jnp.int32, (rank, rank), 0)
        >= lax.broadcasted_iota(jnp.int32, (rank, rank), 1)
    )
    inverse = jnp.where(keep, work[:, rank:], 0.0)
    basis_ref[...] = lax.dot_general(
        sketch_ref[pl.ds(pl.multiple_of(gx * own_rows, own_rows), own_rows), :], inverse,
        (((1,), (1,)), ((), ())), precision=HIGHEST, preferred_element_type=F32,
    )
    return lax.dot_general(
        inverse, sketch_ref[...], (((1,), (1,)), ((), ())),
        precision=HIGHEST, preferred_element_type=F32,
    ).astype(BF16)


def local(n_gx, n_yz, tensor_slabs, slab_counts, column_scale, samples):
    rows, slots, width = tensor_slabs.shape
    rank = samples.shape[1]
    slab_total = column_scale.shape[0]
    n_y = n_yz // CORES
    chunk = rows // n_yz
    own_cols = width // n_gx
    vmem = pl.BlockSpec(memory_space=pltpu.VMEM)
    smem = pl.BlockSpec(memory_space=pltpu.SMEM)
    dma = pltpu.SemaphoreType.DMA
    moves = own_cols % 128 == 0
    every = rows * n_gx
    operands = [slab_counts, jnp.transpose(tensor_slabs, (1, 0, 2)), column_scale, samples]
    exchange = [
        pltpu.VMEM((slots, every, own_cols), BF16), dma((n_gx - 1,)), dma((n_gx - 1,)), dma(())
    ]
    if not moves:
        operands.append(
            jnp.transpose(
                lax.all_to_all(tensor_slabs, "gx", split_axis=2, concat_axis=0, tiled=True),
                (1, 0, 2),
            )
        )
        exchange = []
    basis_factor, core = pl.pallas_call(
        functools.partial(sketch_kernel, n_gx, n_yz, slab_total, moves),
        out_shape=(
            jax.ShapeDtypeStruct((rows, rank), F32),
            jax.ShapeDtypeStruct((slots, rank, own_cols), BF16),
        ),
        in_specs=[smem] + [vmem] * (len(operands) - 1),
        out_specs=(vmem, vmem),
        scratch_shapes=[
            pltpu.VMEM((every, rank), F32),
            pltpu.VMEM((rank, 2 * rank), F32),
            pltpu.VMEM((width, rank), BF16),
            pltpu.VMEM((rows, rank), F32),
            pltpu.VMEM((n_yz - 1, chunk, rank), F32),
            dma((n_yz - 1,)), dma((n_yz - 1,)),
            dma((n_gx - 1,)), dma((n_gx - 1,)),
            dma((max(n_y - 1, 1), n_gx)), dma((max(n_y - 1, 1), n_gx)),
            dma((n_y, n_gx)), dma((n_y, n_gx)),
        ] + exchange,
        compiler_params=pltpu.CompilerParams(
            collective_id=0, has_side_effects=True, vmem_limit_bytes=32 << 20
        ),
    )(*operands)
    return basis_factor, jnp.transpose(core, (1, 0, 2))


def solution(mesh):
    placed = (P("gx", "yz", None), P(), P(), P())
    return jax.shard_map(
        functools.partial(local, mesh.shape["gx"], mesh.shape["yz"]),
        mesh=mesh,
        in_specs=placed,
        out_specs=(P("gx", None), P(None, "yz", "gx")),
        check_vma=False,
    )
```
